32 devices in a mesh: exp: 16 (over z, x, core), tp: 2 (over y).
Axes of the slice: x: 2, y: 2, z: 4, core: 2. Of those that a mesh axis runs over, the one named last changes fastest.
Arguments:
- tokens: bfloat16 [8192, 1024], P(('exp', 'tp')), may hold values from -6 to 6
- gain_attn: float32 [1024], replicated, may hold values from 0.1 to 1.9
- w_query: bfloat16 [1024, 1024], P(None, 'tp'), may hold values from -0.25 to 0.25
- w_key: bfloat16 [1024, 512], P(None, 'tp'), may hold values from -0.25 to 0.25
- w_value: bfloat16 [1024, 512], P(None, 'tp'), may hold values from -0.1875 to 0.1875
- w_out: bfloat16 [1024, 1024], replicated, may hold values from -0.5 to 0.5
- gain_ffn: float32 [1024], replicated, may hold values from 0.1 to 1.9
- w_router: bfloat16 [1024, 32], replicated, may hold values from -0.09375 to 0.09375
- w_gate: bfloat16 [32, 1024, 512], P('exp', None, 'tp'), may hold values from -0.1875 to 0.1875
- w_up: bfloat16 [32, 1024, 512], P('exp', None, 'tp'), may hold values from -0.1875 to 0.1875
- w_down: bfloat16 [32, 512, 1024], P('exp', 'tp'), may hold values from -1 to 1
- segment_ids: int32 [8192], P('exp'), may hold values from 0 to 15, never falling along the last dimension, each value on 1 to 2000 neighbouring positions
- routes: int32 [8192, 8], P(('exp', 'tp')), may hold values from 0 to 31, all different within a row; in each aligned block of 256 rows (0 to 255, 256 to 511, ...) at most 128 rows name the same one
- out_grad: bfloat16 [8192, 1024], P(('exp', 'tp')), may hold values from -6 to 6
Outputs:
- output: bfloat16 [8192, 1024], P(('exp', 'tp'))
- input_grad: float32 [8192, 1024], P(('exp', 'tp'))
- gain_attn_grad: float32 [1024], replicated
- w_query_grad: float32 [1024, 1024], P(None, 'tp')
- w_key_grad: float32 [1024, 512], P(None, 'tp')
- w_value_grad: float32 [1024, 512], P(None, 'tp')
- w_out_grad: float32 [1024, 1024], replicated
- gain_ffn_grad: float32 [1024], replicated
- w_router_grad: float32 [1024, 32], replicated
- w_gate_grad: float32 [32, 1024, 512], P('exp', None, 'tp')
- w_up_grad: float32 [32, 1024, 512], P('exp', None, 'tp')
- w_down_grad: float32 [32, 512, 1024], P('exp', 'tp')
The draws below stay inside these ranges and needn't reach their ends.
Inputs may be any that keep to these rules, and one draw needn't show every extreme that they name: `routes`: each row names 8 different experts. In the rows of one device (aligned blocks of 256 rows) each expert is named by at most 128 rows, a bound that some block reaches. `segment_ids`: never falling along the array; each document number covers 1 to 2000 consecutive tokens, one exactly 2000.
All inputs are finite; a program needn't handle non-finite values.
Results may differ from the reference program's by a relative error of at most 0.023.
Values may be sent and summed in bfloat16 or wider, within the bound.
A program may use at most 192 MiB of HBM per device.

```python
import math
import jax
import jax.numpy as jnp
import numpy as np
from jax import lax

D = 1024
HQ = 16
HK = 8
HEAD = 64
EXPERTS = 32
TOP = 8
FF = 512
TOK_DEV = 256
DOC_MOST = 2000
CAP = 128
SEQ = 512
TOKENS = 8192


def shard_levels(key, dims, split, smallest, top_value):
    def one(axis_at, blocks):
        heights = jax.random.uniform(jax.random.fold_in(jax.random.fold_in(key, 6), axis_at), (blocks,), jnp.float32, smallest / len(split), top_value / len(split))
        return jnp.repeat(jnp.exp(heights), dims[axis_at] // blocks).reshape((-1,) + (1,) * (len(dims) - axis_at - 1))

    gain = one(*split[0])
    for cut in split[1:]:
        gain = gain * one(*cut)
    return gain


def split_up(number_of, total, most, lean):
    loads = [(1 << 20) // math.isqrt(grade ** lean) + 1 for grade in range(2, number_of + 1)]
    rest, holding = total - most - (number_of - 1), [1] * (number_of - 1)
    while rest > 0:
        candidates = [i for i in range(number_of - 1) if holding[i] < most]
        pool, remaining = sum([loads[i] for i in candidates]), rest
        for i in candidates:
            extra = min(most - holding[i], max(1, remaining * loads[i] // pool), rest)
            holding[i] = holding[i] + extra
            rest = rest - extra
    return np.array([most] + holding)


def ragged_sizes(key, count, total, limit, slope):
    if count == 2:
        one = jax.random.randint(key, (), max(1, total - limit), min(limit, total - 1) + 1)
        return jnp.stack([one, total - one])
    tallies = jnp.asarray(split_up(count, total, limit, slope), jnp.int32)
    pairs = (count - 1) // 2
    giver, taker = tallies[1:1 + 2 * pairs:2], tallies[2:2 + 2 * pairs:2]
    margin = jnp.minimum(giver - 1, limit - taker)
    shifted = jax.random.randint(jax.random.fold_in(key, 1), (pairs,), 0, 1 << 20) % (margin + 1)
    tallies = tallies.at[1:1 + 2 * pairs:2].set(giver - shifted).at[2:2 + 2 * pairs:2].set(taker + shifted)
    return tallies[jax.random.permutation(jax.random.fold_in(key, 2), count)]


def routed_block(rng, own, number, rows, count, top, most, slope):
    sequence = jax.random.permutation(rng, count)
    crowded, ordinary = portions_of(count, rows * top, most, slope, True), portions_of(count, rows * top, most, slope, False)
    places = jnp.arange(count)

    def named(lengths, rotation):
        used = int((lengths > 0).sum())
        fixed = max(1, used // 4)
        shifted = fixed + (places - fixed + rotation * (used - fixed)) % max(1, count - fixed)
        return jnp.zeros((count,), jnp.int32).at[sequence[jnp.where(places < fixed, places, shifted)]].set(jnp.asarray(lengths, jnp.int32))

    lengths = jnp.where(number % 4 == 0, named(crowded, number // 4), named(ordinary, number - number // 4 - 1))
    mixed = jax.random.permutation(jax.random.fold_in(own, 3), count)
    source_of, sink = mixed[0:count // 2 * 2:2], mixed[1:count // 2 * 2:2]
    room = jnp.minimum(lengths[source_of] - 1, most - lengths[sink]) // 2
    room = jnp.where((source_of == sequence[0]) | (sink == sequence[0]) | (lengths[sink] == 0), 0, jnp.maximum(room, 0))
    shifted = jax.random.randint(jax.random.fold_in(own, 4), (count // 2,), 0, 1 << 20) % (room + 1)
    lengths = lengths.at[source_of].add(-shifted).at[sink].add(shifted)
    members = jnp.searchsorted(jnp.cumsum(lengths), jnp.arange(rows * top), side="right").astype(jnp.int32)
    table = members.reshape(top, rows).T
    table = table[jax.random.permutation(jax.random.fold_in(own, 1), rows)]
    rotation = jax.random.randint(jax.random.fold_in(own, 2), (rows, 1), 0, top)
    return jnp.take_along_axis(table, (jnp.arange(top)[None, :] + rotation) % top, axis=1)


def portions_of(amount, total, bound, skew, full):
    portions = [(1 << 20) // math.isqrt(rank ** skew) + 1 for rank in range(1, amount + 1)]
    largest = bound if full else min(bound, max(-(-total // amount), total * portions[0] // sum(portions)))
    least = 1 if total - largest >= amount - 1 else 0
    counts, surplus = [largest] + [least] * (amount - 1), total - largest - least * (amount - 1)
    while surplus > 0:
        movable = [i for i in range(1, amount) if counts[i] < largest] or [i for i in range(1, amount) if counts[i] < bound]
        mass, budget = sum([portions[i] for i in movable]), surplus
        for i in movable:
            addition = min(bound - counts[i], max(1, budget * portions[i] // mass), surplus)
            counts[i] = counts[i] + addition
            surplus = surplus - addition
    return np.array(counts)


def scatter_about(stream_key, extent, deviation, reach, cuts=(), kind=jnp.bfloat16):
    values = jax.random.normal(stream_key, extent, jnp.float32) * deviation
    if len(cuts) > 0:
        values = shard_levels(stream_key, extent, cuts, -0.22, 0.18) * values
    return jnp.clip(values, min=-reach, max=reach).astype(kind)


def setup_inputs(seed: int = 0) -> dict:
    key_of = jax.random.split(jax.random.key(seed), 15)
    tokens = scatter_about(key_of[0], (TOKENS, D), 1.0, 6.0, ((0, 32),))
    gain_attn = jnp.clip(1.0 + 0.18 * jax.random.normal(key_of[1], (D,), jnp.float32), 0.1, 1.9)
    w_query = scatter_about(key_of[2], (D, HQ * HEAD), (D // 2) ** -0.5, 0.25, ((1, 2),))
    w_key = scatter_about(key_of[3], (D, HK * HEAD), (D // 2) ** -0.5, 0.25, ((1, 2),))
    w_value = scatter_about(key_of[4], (D, HK * HEAD), D ** -0.5, 0.1875, ((1, 2),))
    w_out = scatter_about(key_of[5], (HQ * HEAD, D), (D // 8) ** -0.5, 0.5)
    gain_ffn = jnp.clip(1.0 + 0.18 * jax.random.normal(key_of[6], (D,), jnp.float32), 0.1, 1.9)
    w_router = scatter_about(key_of[7], (D, EXPERTS), (4 * D) ** -0.5, 0.09375)
    w_gate = scatter_about(key_of[8], (EXPERTS, D, FF), D ** -0.5, 0.1875, ((0, 16), (2, 2)))
    w_up = scatter_about(key_of[9], (EXPERTS, D, FF), D ** -0.5, 0.1875, ((0, 16), (2, 2)))
    w_down = scatter_about(key_of[10], (EXPERTS, FF, D), (FF // 16) ** -0.5, 1.0, ((0, 16), (1, 2)))
    segment_ids = jnp.searchsorted(jnp.cumsum(ragged_sizes(key_of[11], 4 * TOKENS // DOC_MOST, TOKENS, DOC_MOST, 2)), jnp.arange(TOKENS), side="right").astype(jnp.int32)
    routes_keys = jax.random.split(jax.random.fold_in(key_of[12], 1), TOKENS // TOK_DEV)
    routes_turns = jax.random.permutation(jax.random.fold_in(key_of[12], 3), TOKENS // TOK_DEV)
    routes = jax.vmap(lambda own, number: routed_block(jax.random.fold_in(key_of[12], 2), own, number, TOK_DEV, EXPERTS, TOP, CAP, 1))(routes_keys, routes_turns).reshape((TOKENS, TOP))
    out_grad = scatter_about(key_of[13], (TOKENS, D), 1.0, 6.0, ((0, 32),))
    return dict(tokens=tokens, gain_attn=gain_attn, w_query=w_query, w_key=w_key, w_value=w_value, w_out=w_out, gain_ffn=gain_ffn, w_router=w_router, w_gate=w_gate, w_up=w_up, w_down=w_down, segment_ids=segment_ids, routes=routes, out_grad=out_grad)


epsilon = 1e-06
base_theta = 10000.0
precise = lax.Precision.HIGHEST

@jax.custom_vjp
def low(v):
    return lax.optimization_barrier(v.astype(jnp.bfloat16)).astype(jnp.float32)

@jax.custom_vjp
def low_back(v):
    return v

def low_keep(v):
    return (low(v), None)

def low_pass(kept, grad):
    return (grad,)

def back_keep(v):
    return (v, None)

def back_low(kept, grad):
    return (low(grad),)
low.defvjp(low_keep, low_pass)
low_back.defvjp(back_keep, back_low)

def matmul(left, right):
    return jnp.dot(left, right, precision=precise)

def rms_unit(values):
    return values * lax.rsqrt(lax.optimization_barrier(jnp.mean(values * values, axis=-1, keepdims=True)) + epsilon)

def doc_positions(seg_rows):
    indices = jnp.arange(seg_rows.shape[-1], dtype=jnp.int32)
    previous = jnp.concatenate([seg_rows[..., :1], seg_rows[..., :-1]], axis=-1)
    starts = (indices == 0) | (seg_rows != previous)
    latest = lax.cummax(jnp.where(starts, indices, 0), axis=seg_rows.ndim - 1)
    return indices - latest

def rope_tables(positions):
    halves = HEAD // 2
    frequency = base_theta ** (-2.0 * jnp.arange(halves, dtype=jnp.float32) / HEAD)
    angles = positions.astype(jnp.float32)[:, None] * frequency[None, :]
    angles = jnp.concatenate([angles, angles], axis=1)
    return (jnp.cos(angles)[:, None, :], jnp.sin(angles)[:, None, :])

def rotate(values, cos_table, sin_table):
    halves = values.shape[-1] // 2
    turned = jnp.concatenate([-values[..., halves:], values[..., :halves]], axis=-1)
    return values * cos_table + turned * sin_table

def attend(seq_item):
    queries, key_rows, value_rows, seg_rows = seq_item
    length = queries.shape[0]
    grouped = queries.reshape(length, HK, HQ // HK, HEAD)
    scores = jnp.einsum('qhgd,khd->hgqk', grouped, key_rows, precision=precise) * HEAD ** (-0.5)
    scores = low_back(scores)
    indices = jnp.arange(length)
    allowed = (indices[:, None] >= indices[None, :]) & (seg_rows[:, None] == seg_rows[None, :])
    scores = jnp.where(allowed, scores, -1e+30)
    highest = lax.optimization_barrier(jnp.max(scores, axis=-1, keepdims=True))
    weights = jnp.exp(scores - highest)
    shares = low(weights / lax.optimization_barrier(jnp.sum(weights, axis=-1, keepdims=True)))
    attended = jnp.einsum('hgqk,khd->qhgd', shares, value_rows, precision=precise)
    return attended.reshape(length, HQ * HEAD)

def expert_block(normed_rows, logit_rows, route_rows, gate_weight, up_weight, down_weight):
    count_rows = normed_rows.shape[0]
    flat_routes = route_rows.reshape(-1)
    expert_ids = jnp.arange(EXPERTS, dtype=jnp.int32)
    onehot = (flat_routes[:, None] == expert_ids[None, :]).astype(jnp.int32)
    rank_rows = lax.optimization_barrier(jnp.sum((jnp.cumsum(onehot, axis=0) - onehot) * onehot, axis=1))
    slot_index = flat_routes * CAP + rank_rows
    owner_rows = jnp.arange(count_rows * TOP, dtype=jnp.int32) // TOP
    source_rows = jnp.zeros((EXPERTS * CAP,), jnp.int32).at[slot_index].set(owner_rows)
    filled = jnp.zeros((EXPERTS * CAP,), jnp.int32).at[slot_index].set(1)
    packed = jnp.where(filled[:, None] > 0, normed_rows[source_rows], 0.0)
    packed = low_back(packed).reshape(EXPERTS, CAP, normed_rows.shape[1])
    gate_pre = low_back(jnp.einsum('ecd,edf->ecf', packed, gate_weight, precision=precise))
    up_pre = low_back(jnp.einsum('ecd,edf->ecf', packed, up_weight, precision=precise))
    inner_act = low(gate_pre * jax.nn.sigmoid(gate_pre) * up_pre)
    result = low(low_back(jnp.einsum('ecf,efd->ecd', inner_act, down_weight, precision=precise)))
    result = result.reshape(EXPERTS * CAP, -1)
    picked = result[slot_index].reshape(count_rows, TOP, -1)
    route_hits = route_rows[:, :, None] == expert_ids[None, None, :]
    chosen = lax.optimization_barrier(jnp.sum(jnp.where(route_hits, logit_rows[:, None, :], 0.0), axis=2))
    highest = lax.optimization_barrier(jnp.max(chosen, axis=1, keepdims=True))
    weights = jnp.exp(chosen - highest)
    gate_shares = weights / lax.optimization_barrier(jnp.sum(weights, axis=1, keepdims=True))
    return lax.optimization_barrier(jnp.sum(gate_shares[:, :, None] * picked, axis=1))

def block_forward(tokens, gain_attn, w_query, w_key, w_value, w_out, gain_ffn, w_router, w_gate, w_up, w_down, segment_ids, routes):
    token_count = tokens.shape[0]
    seq_rows = segment_ids.reshape(token_count // SEQ, SEQ)
    cos_table, sin_table = rope_tables(doc_positions(seq_rows).reshape(-1))
    normed = low(rms_unit(tokens) * gain_attn)
    queries = low(rotate(low_back(matmul(normed, w_query)).reshape(token_count, HQ, HEAD), cos_table, sin_table))
    key_rows = low(rotate(low_back(matmul(normed, w_key)).reshape(token_count, HK, HEAD), cos_table, sin_table))
    value_rows = low(low_back(matmul(normed, w_value))).reshape(token_count, HK, HEAD)
    attended = lax.map(jax.checkpoint(attend), (queries.reshape(-1, SEQ, HQ, HEAD), key_rows.reshape(-1, SEQ, HK, HEAD), value_rows.reshape(-1, SEQ, HK, HEAD), seq_rows))
    head_rows = low(low_back(attended.reshape(token_count, HQ * HEAD)))
    hidden = tokens + low_back(matmul(head_rows, w_out))
    normed_ffn = low(rms_unit(hidden) * gain_ffn)
    logits = low_back(matmul(normed_ffn, w_router))

    def block_step(seq_item):
        return expert_block(seq_item[0], seq_item[1], seq_item[2], w_gate, w_up, w_down)
    mixture = lax.map(jax.checkpoint(block_step), (normed_ffn.reshape(-1, TOK_DEV, D), logits.reshape(-1, TOK_DEV, EXPERTS), routes.reshape(-1, TOK_DEV, TOP)))
    return hidden + mixture.reshape(token_count, -1)

def reference(tokens, gain_attn, w_query, w_key, w_value, w_out, gain_ffn, w_router, w_gate, w_up, w_down, segment_ids, routes, out_grad):

    def forward(tokens, gain_attn, w_query, w_key, w_value, w_out, gain_ffn, w_router, w_gate, w_up, w_down):
        return block_forward(tokens, gain_attn, w_query, w_key, w_value, w_out, gain_ffn, w_router, w_gate, w_up, w_down, segment_ids, routes)
    output, pullback = jax.vjp(forward, tokens.astype(jnp.float32), gain_attn.astype(jnp.float32), w_query.astype(jnp.float32), w_key.astype(jnp.float32), w_value.astype(jnp.float32), w_out.astype(jnp.float32), gain_ffn.astype(jnp.float32), w_router.astype(jnp.float32), w_gate.astype(jnp.float32), w_up.astype(jnp.float32), w_down.astype(jnp.float32))
    grads = pullback(out_grad.astype(jnp.float32))
    return (output.astype(jnp.bfloat16), grads[0], grads[1], grads[2], grads[3], grads[4], grads[5], grads[6], grads[7], grads[8], grads[9], grads[10])
```

```python
import jax
import jax.numpy as jnp
from jax import lax
from jax.sharding import PartitionSpec as P

HEAD = 64
SEQ_LEN = 512
CAP = 128


epsilon = 1e-06
base_theta = 10000.0


def contract(left, right, left_dim, right_dim):
    return lax.dot_general(
        left, right, (((left_dim,), (right_dim,)), ((), ())), preferred_element_type=jnp.float32
    )


def doc_positions(seg_rows):
    indices = jnp.arange(seg_rows.shape[-1], dtype=jnp.int32)
    previous = jnp.concatenate([seg_rows[..., :1], seg_rows[..., :-1]], axis=-1)
    starts = (indices == 0) | (seg_rows != previous)
    latest = lax.cummax(jnp.where(starts, indices, 0), axis=seg_rows.ndim - 1)
    return indices - latest


def rope_tables(positions, head_dim):
    halves = head_dim // 2
    frequency = base_theta ** (-2.0 * jnp.arange(halves, dtype=jnp.float32) / head_dim)
    angles = positions.astype(jnp.float32)[:, None] * frequency[None, :]
    angles = jnp.concatenate([angles, angles], axis=1)
    return (jnp.cos(angles)[:, None, :], jnp.sin(angles)[:, None, :])


def rotate(values, cos_table, sin_table):
    halves = values.shape[-1] // 2
    turned = jnp.concatenate([-values[..., halves:], values[..., :halves]], axis=-1)
    return values * cos_table + turned * sin_table


def rotate_back(grads, cos_table, sin_table):
    halves = grads.shape[-1] // 2
    scaled = grads * sin_table
    return grads * cos_table + jnp.concatenate(
        [scaled[..., halves:], -scaled[..., :halves]], axis=-1
    )


def masked_scores(queries, key_rows, seg_rows):
    length, kv_heads, head_dim = key_rows.shape
    grouped = queries.reshape(length, kv_heads, -1, head_dim)
    raw_scores = jnp.einsum(
        "qhgd,khd->hgqk", grouped, key_rows, preferred_element_type=jnp.float32
    ) * head_dim ** (-0.5)
    indices = jnp.arange(length)
    allowed = (indices[:, None] >= indices[None, :]) & (seg_rows[:, None] == seg_rows[None, :])
    return (jnp.where(allowed, raw_scores, -1e30), grouped)


def attend_forward(seq_item):
    queries, key_rows, value_rows, seg_rows = seq_item
    scores, grouped = masked_scores(queries, key_rows, seg_rows)
    highest = jnp.max(scores, axis=-1, keepdims=True)
    weights = jnp.exp(scores - highest)
    totals = jnp.sum(weights, axis=-1, keepdims=True)
    shares = (weights / totals).astype(jnp.bfloat16)
    attended = jnp.einsum("hgqk,khd->qhgd", shares, value_rows, preferred_element_type=jnp.float32)
    return (attended.reshape(queries.shape[0], -1), highest + jnp.log(totals))


def attend_backward(seq_item):
    queries, key_rows, value_rows, seg_rows, log_total, head_grad = seq_item
    scores, grouped = masked_scores(queries, key_rows, seg_rows)
    factor = key_rows.shape[2] ** (-0.5)
    shares = jnp.exp(scores - log_total)
    grad_grouped = head_grad.reshape(grouped.shape)
    share_grad = jnp.einsum(
        "qhgd,khd->hgqk", grad_grouped, value_rows, preferred_element_type=jnp.float32
    )
    row_dot = jnp.sum(shares * share_grad, axis=-1, keepdims=True)
    score_grad = (shares * (share_grad - row_dot)).astype(jnp.bfloat16)
    query_grad = (
        jnp.einsum("hgqk,khd->qhgd", score_grad, key_rows, preferred_element_type=jnp.float32)
        * factor
    )
    key_grad = (
        jnp.einsum("hgqk,qhgd->khd", score_grad, grouped, preferred_element_type=jnp.float32)
        * factor
    )
    value_grad = jnp.einsum(
        "hgqk,qhgd->khd",
        shares.astype(jnp.bfloat16),
        grad_grouped,
        preferred_element_type=jnp.float32,
    )
    return (query_grad.reshape(queries.shape[0], -1), key_grad, value_grad)


def dense_gates(logits, routes, expert_ids):
    hits = jnp.any(routes[:, :, None] == expert_ids[None, None, :], axis=1)
    chosen = jnp.where(hits, logits, -jnp.inf)
    weights = jnp.exp(chosen - jnp.max(chosen, axis=1, keepdims=True))
    return weights / jnp.sum(weights, axis=1, keepdims=True)


def shards(
    tokens,
    gain_attn,
    w_query,
    w_key,
    w_value,
    w_out,
    gain_ffn,
    w_router,
    w_gate,
    w_up,
    w_down,
    segment_ids,
    routes,
    out_grad,
):
    tok_rows, width = tokens.shape
    group_rows = segment_ids.shape[0]
    seq_len = SEQ_LEN
    seq_count = group_rows // seq_len
    query_cols = w_query.shape[1]
    kv_cols = w_key.shape[1]
    head_dim = HEAD
    tp_index = lax.axis_index("tp")
    expert_count = w_router.shape[1]
    capacity = CAP
    top_count = routes.shape[1]
    local_experts = w_gate.shape[0]
    owner_count = lax.axis_size("exp")
    gate_full, up_full, down_full = (
        lax.all_gather(w_gate, "tp", axis=2, tiled=True),
        lax.all_gather(w_up, "tp", axis=2, tiled=True),
        lax.all_gather(w_down, "tp", axis=1, tiled=True),
    )
    exp_index = lax.axis_index("exp")
    routes_all = lax.all_gather(routes, "exp", axis=0, tiled=True)
    og_all = lax.all_gather(out_grad, "exp", axis=0, tiled=True)
    own_ids = exp_index * local_experts + jnp.arange(local_experts, dtype=jnp.int32)
    own_hits = jnp.any(
        routes_all.T.reshape(1, top_count, owner_count, tok_rows)
        == own_ids[:, None, None, None],
        axis=1,
    )
    tok_ids = jnp.arange(tok_rows, dtype=jnp.int32)
    earlier = (tok_ids[:, None] < tok_ids[None, :]).astype(jnp.bfloat16)
    ranks = jnp.einsum(
        "usr,rt->ust", own_hits.astype(jnp.bfloat16), earlier, preferred_element_type=jnp.float32
    ).astype(jnp.int32)
    ranks = jnp.where(own_hits, ranks, -1)
    dispatch = (
        ranks[:, :, None, :] == jnp.arange(capacity, dtype=jnp.int32)[None, None, :, None]
    ).astype(jnp.bfloat16)
    og_packed = jnp.einsum(
        "usct,std->uscd",
        dispatch,
        og_all.reshape(owner_count, tok_rows, width),
        preferred_element_type=jnp.float32,
    ).astype(jnp.bfloat16).reshape(local_experts, -1, width)
    source = tokens.astype(jnp.float32)
    scale_one = lax.rsqrt(jnp.mean(source * source, axis=1, keepdims=True) + epsilon)
    unit_one = source * scale_one
    normed = (unit_one * gain_attn).astype(jnp.bfloat16)
    gathered = lax.all_gather(normed, "tp", axis=0, tiled=True)
    w_proj = jnp.concatenate([w_query, w_key, w_value], axis=1)
    projected = jnp.dot(gathered, w_proj, preferred_element_type=jnp.float32)
    seq_rows = segment_ids.reshape(seq_count, seq_len)
    cos_table, sin_table = rope_tables(doc_positions(seq_rows).reshape(-1), head_dim)
    queries = rotate(
        projected[:, :query_cols].reshape(group_rows, -1, head_dim), cos_table, sin_table
    ).astype(jnp.bfloat16)
    key_rows = rotate(
        projected[:, query_cols : query_cols + kv_cols].reshape(group_rows, -1, head_dim),
        cos_table,
        sin_table,
    ).astype(jnp.bfloat16)
    value_rows = (
        projected[:, query_cols + kv_cols :].astype(jnp.bfloat16).reshape(group_rows, -1, head_dim)
    )
    query_seqs = queries.reshape(seq_count, seq_len, -1, head_dim)
    key_seqs = key_rows.reshape(seq_count, seq_len, -1, head_dim)
    value_seqs = value_rows.reshape(seq_count, seq_len, -1, head_dim)
    attended, log_total = lax.map(attend_forward, (query_seqs, key_seqs, value_seqs, seq_rows))
    head_rows = attended.reshape(group_rows, query_cols).astype(jnp.bfloat16)
    out_local = lax.dynamic_slice_in_dim(w_out, tp_index * query_cols, query_cols, 0)
    part_rows = head_rows
    branch = lax.psum_scatter(
        jnp.dot(part_rows, out_local, preferred_element_type=jnp.float32),
        "tp",
        scatter_dimension=0,
        tiled=True,
    )
    hidden = source + branch
    scale_two = lax.rsqrt(jnp.mean(hidden * hidden, axis=1, keepdims=True) + epsilon)
    unit_two = hidden * scale_two
    normed_ffn = (unit_two * gain_ffn).astype(jnp.bfloat16)
    logits = jnp.dot(normed_ffn, w_router, preferred_element_type=jnp.float32)
    expert_ids = jnp.arange(expert_count, dtype=jnp.int32)
    gates = dense_gates(logits, routes, expert_ids)
    x_all = lax.all_gather(normed_ffn, "exp", axis=0, tiled=True).reshape(
        owner_count, tok_rows, width
    )
    logits_all = jnp.einsum("std,de->ste", x_all, w_router, preferred_element_type=jnp.float32)
    gates_all = dense_gates(
        logits_all.reshape(-1, expert_count), routes_all, expert_ids
    ).reshape(owner_count, tok_rows, owner_count, local_experts)
    own_gates = lax.dynamic_index_in_dim(gates_all, exp_index, 2, keepdims=False)
    slot_gates = jnp.einsum(
        "usct,stu->usc", dispatch, own_gates, precision=lax.Precision.HIGHEST,
        preferred_element_type=jnp.float32,
    )
    received = jnp.einsum(
        "usct,std->uscd", dispatch, x_all, preferred_element_type=jnp.float32
    ).astype(jnp.bfloat16).reshape(local_experts, -1, width)
    slot_gates = slot_gates.reshape(local_experts, -1)
    gate_pre = jnp.einsum("umd,udf->umf", received, gate_full, preferred_element_type=jnp.float32)
    up_pre = jnp.einsum("umd,udf->umf", received, up_full, preferred_element_type=jnp.float32)
    sigmoid_gate = jax.nn.sigmoid(gate_pre)
    inner_act = (gate_pre * sigmoid_gate * up_pre).astype(jnp.bfloat16)
    result = jnp.einsum(
        "umf,ufd->umd", inner_act, down_full, preferred_element_type=jnp.float32
    ).astype(jnp.bfloat16).astype(jnp.float32)
    weighted = (slot_gates[..., None] * result).astype(jnp.bfloat16)
    mixture_part = jnp.einsum(
        "usct,uscd->std",
        dispatch,
        weighted.reshape(local_experts, owner_count, capacity, width),
        preferred_element_type=jnp.float32,
    ).astype(jnp.bfloat16)
    mixture = lax.psum_scatter(
        mixture_part.reshape(-1, width), "exp", scatter_dimension=0, tiled=True
    ).astype(jnp.float32)
    output = (hidden + mixture).astype(jnp.bfloat16)
    share_slots = jnp.sum(result * og_packed.astype(jnp.float32), axis=2)
    share_back = jnp.einsum(
        "usct,usc->sut", dispatch, share_slots.reshape(local_experts, owner_count, capacity),
        precision=lax.Precision.HIGHEST, preferred_element_type=jnp.float32,
    )
    share_grad = (
        lax.all_to_all(share_back, "exp", split_axis=0, concat_axis=0, tiled=True)
        .reshape(expert_count, tok_rows)
        .T
    )
    arrived = (slot_gates[..., None] * og_packed.astype(jnp.float32)).astype(jnp.bfloat16)
    inner_grad = jnp.einsum("umd,ufd->umf", arrived, down_full, preferred_element_type=jnp.float32)
    gate_grad = (
        inner_grad * up_pre * sigmoid_gate * (1.0 + gate_pre * (1.0 - sigmoid_gate))
    ).astype(jnp.bfloat16)
    up_grad = (inner_grad * gate_pre * sigmoid_gate).astype(jnp.bfloat16)
    back_rows = (
        jnp.einsum("umf,udf->umd", gate_grad, gate_full, preferred_element_type=jnp.float32)
        + jnp.einsum("umf,udf->umd", up_grad, up_full, preferred_element_type=jnp.float32)
    ).astype(jnp.bfloat16)
    grad_part = jnp.einsum(
        "usct,uscd->std",
        dispatch,
        back_rows.reshape(local_experts, owner_count, capacity, width),
        preferred_element_type=jnp.float32,
    ).astype(jnp.bfloat16)
    ffn_grad = lax.psum_scatter(
        grad_part.reshape(-1, width), "exp", scatter_dimension=0, tiled=True
    ).astype(jnp.float32)
    down_part = jnp.einsum("umf,umd->ufd", inner_act, arrived, preferred_element_type=jnp.float32)
    gate_part = jnp.einsum("umd,umf->udf", received, gate_grad, preferred_element_type=jnp.float32)
    up_part = jnp.einsum("umd,umf->udf", received, up_grad, preferred_element_type=jnp.float32)
    logit_grad = (
        gates * (share_grad - jnp.sum(gates * share_grad, axis=1, keepdims=True))
    ).astype(jnp.bfloat16)
    router_part = contract(normed_ffn, logit_grad, 0, 0)
    ffn_grad = ffn_grad + contract(logit_grad, w_router, 1, 1)
    ffn_part = jnp.sum(ffn_grad * unit_two, axis=0)
    unit_grad_two = ffn_grad * gain_ffn
    hidden_grad = out_grad.astype(jnp.float32) + scale_two * (
        unit_grad_two - unit_two * jnp.mean(unit_grad_two * unit_two, axis=1, keepdims=True)
    )
    branch_low = hidden_grad.astype(jnp.bfloat16)
    part_rows = lax.all_gather(branch_low, "tp", axis=0, tiled=True)
    update = contract(part_rows, out_local, 1, 1)
    grads_heads = update
    grads_heads, out_rows = (grads_heads, contract(head_rows, part_rows, 0, 0))
    head_grad = grads_heads.astype(jnp.bfloat16)
    out_weight_grad = lax.all_gather(
        lax.psum(out_rows.astype(jnp.bfloat16), "exp"), "tp", axis=0, tiled=True
    ).astype(jnp.float32)
    query_grad, key_grad, value_grad = lax.map(
        attend_backward,
        (
            query_seqs,
            key_seqs,
            value_seqs,
            seq_rows,
            log_total,
            head_grad.reshape(seq_count, seq_len, query_cols),
        ),
    )
    query_grad = rotate_back(query_grad.reshape(group_rows, -1, head_dim), cos_table, sin_table)
    key_grad = rotate_back(key_grad.reshape(group_rows, -1, head_dim), cos_table, sin_table)
    proj_grad = jnp.concatenate(
        [
            query_grad.reshape(group_rows, -1),
            key_grad.reshape(group_rows, -1),
            value_grad.reshape(group_rows, -1),
        ],
        axis=1,
    ).astype(jnp.bfloat16)
    proj_part = contract(gathered, proj_grad, 0, 0)
    part_rows = proj_grad
    normed_grad = lax.psum_scatter(
        contract(part_rows, w_proj, 1, 1).astype(jnp.bfloat16),
        "tp",
        scatter_dimension=0,
        tiled=True,
    ).astype(jnp.float32)
    attn_part = jnp.sum(normed_grad * unit_one, axis=0)
    unit_grad_one = normed_grad * gain_attn
    input_grad = hidden_grad + scale_one * (
        unit_grad_one - unit_one * jnp.mean(unit_grad_one * unit_one, axis=1, keepdims=True)
    )
    gate_weight_grad, up_weight_grad, down_weight_grad = (
        lax.psum_scatter(
            gate_part.astype(jnp.bfloat16), "tp", scatter_dimension=2, tiled=True
        ).astype(jnp.float32),
        lax.psum_scatter(
            up_part.astype(jnp.bfloat16), "tp", scatter_dimension=2, tiled=True
        ).astype(jnp.float32),
        lax.psum_scatter(
            down_part.astype(jnp.bfloat16), "tp", scatter_dimension=1, tiled=True
        ).astype(jnp.float32),
    )
    query_weight_grad, key_weight_grad, value_weight_grad = (
        lax.psum(proj_part[:, :query_cols].astype(jnp.bfloat16), "exp").astype(jnp.float32),
        lax.psum(
            proj_part[:, query_cols : query_cols + kv_cols].astype(jnp.bfloat16), "exp"
        ).astype(jnp.float32),
        lax.psum(proj_part[:, query_cols + kv_cols :].astype(jnp.bfloat16), "exp").astype(
            jnp.float32
        ),
    )
    attn_gain_grad, ffn_gain_grad, router_grad = lax.psum(
        (attn_part, ffn_part, router_part), ("exp", "tp")
    )
    return (
        output,
        input_grad,
        attn_gain_grad,
        query_weight_grad,
        key_weight_grad,
        value_weight_grad,
        out_weight_grad,
        ffn_gain_grad,
        router_grad,
        gate_weight_grad,
        up_weight_grad,
        down_weight_grad,
    )


def solution(mesh):
    in_specs = (
        P(("exp", "tp"), None),
        P(),
        P(None, "tp"),
        P(None, "tp"),
        P(None, "tp"),
        P(),
        P(),
        P(),
        P("exp", None, "tp"),
        P("exp", None, "tp"),
        P("exp", "tp", None),
        P("exp"),
        P(("exp", "tp"), None),
        P(("exp", "tp"), None),
    )
    out_specs = (
        P(("exp", "tp"), None),
        P(("exp", "tp"), None),
        P(),
        P(None, "tp"),
        P(None, "tp"),
        P(None, "tp"),
        P(),
        P(),
        P(),
        P("exp", None, "tp"),
        P("exp", None, "tp"),
        P("exp", "tp", None),
    )
    return jax.shard_map(shards, mesh=mesh, in_specs=in_specs, out_specs=out_specs, check_vma=False)
```

```python
import jax
import jax.numpy as jnp
from jax import lax
from jax.sharding import PartitionSpec as P

HEAD = 64
SEQ_LEN = 512
CAP = 128


epsilon = 1e-06
base_theta = 10000.0


def contract(left, right, left_dim, right_dim):
    return lax.dot_general(
        left, right, (((left_dim,), (right_dim,)), ((), ())), preferred_element_type=jnp.float32
    )


def doc_positions(seg_rows):
    indices = jnp.arange(seg_rows.shape[-1], dtype=jnp.int32)
    previous = jnp.concatenate([seg_rows[..., :1], seg_rows[..., :-1]], axis=-1)
    starts = (indices == 0) | (seg_rows != previous)
    latest = lax.cummax(jnp.where(starts, indices, 0), axis=seg_rows.ndim - 1)
    return indices - latest


def rope_tables(positions, head_dim):
    halves = head_dim // 2
    frequency = base_theta ** (-2.0 * jnp.arange(halves, dtype=jnp.float32) / head_dim)
    angles = positions.astype(jnp.float32)[:, None] * frequency[None, :]
    angles = jnp.concatenate([angles, angles], axis=1)
    return (jnp.cos(angles)[:, None, :], jnp.sin(angles)[:, None, :])


def rotate(values, cos_table, sin_table):
    halves = values.shape[-1] // 2
    turned = jnp.concatenate([-values[..., halves:], values[..., :halves]], axis=-1)
    return values * cos_table + turned * sin_table


def rotate_back(grads, cos_table, sin_table):
    halves = grads.shape[-1] // 2
    scaled = grads * sin_table
    return grads * cos_table + jnp.concatenate(
        [scaled[..., halves:], -scaled[..., :halves]], axis=-1
    )


def masked_scores(queries, key_rows, seg_rows):
    length, kv_heads, head_dim = key_rows.shape
    grouped = queries.reshape(length, kv_heads, -1, head_dim)
    raw_scores = jnp.einsum(
        "qhgd,khd->hgqk", grouped, key_rows, preferred_element_type=jnp.float32
    ) * head_dim ** (-0.5)
    indices = jnp.arange(length)
    allowed = (indices[:, None] >= indices[None, :]) & (seg_rows[:, None] == seg_rows[None, :])
    return (jnp.where(allowed, raw_scores, -1e30), grouped)


def attend_forward(seq_item):
    queries, key_rows, value_rows, seg_rows = seq_item
    scores, grouped = masked_scores(queries, key_rows, seg_rows)
    highest = jnp.max(scores, axis=-1, keepdims=True)
    weights = jnp.exp(scores - highest)
    totals = jnp.sum(weights, axis=-1, keepdims=True)
    shares = (weights / totals).astype(jnp.bfloat16)
    attended = jnp.einsum("hgqk,khd->qhgd", shares, value_rows, preferred_element_type=jnp.float32)
    return (attended.reshape(queries.shape[0], -1), highest + jnp.log(totals))


def attend_backward(seq_item):
    queries, key_rows, value_rows, seg_rows, log_total, head_grad = seq_item
    scores, grouped = masked_scores(queries, key_rows, seg_rows)
    factor = key_rows.shape[2] ** (-0.5)
    shares = jnp.exp(scores - log_total)
    grad_grouped = head_grad.reshape(grouped.shape)
    share_grad = jnp.einsum(
        "qhgd,khd->hgqk", grad_grouped, value_rows, preferred_element_type=jnp.float32
    )
    row_dot = jnp.sum(shares * share_grad, axis=-1, keepdims=True)
    score_grad = (shares * (share_grad - row_dot)).astype(jnp.bfloat16)
    query_grad = (
        jnp.einsum("hgqk,khd->qhgd", score_grad, key_rows, preferred_element_type=jnp.float32)
        * factor
    )
    key_grad = (
        jnp.einsum("hgqk,qhgd->khd", score_grad, grouped, preferred_element_type=jnp.float32)
        * factor
    )
    value_grad = jnp.einsum(
        "hgqk,qhgd->khd",
        shares.astype(jnp.bfloat16),
        grad_grouped,
        preferred_element_type=jnp.float32,
    )
    return (query_grad.reshape(queries.shape[0], -1), key_grad, value_grad)


def tp_blocks(block):
    count = lax.axis_size("tp")
    return [block] + [
        lax.ppermute(block, "tp", [(j, (j - k) % count) for j in range(count)])
        for k in range(1, count)
    ]


def tp_sum(parts):
    count = lax.axis_size("tp")
    total = parts[0].astype(jnp.float32)
    for k in range(1, count):
        moved = lax.ppermute(parts[k], "tp", [(j, (j + k) % count) for j in range(count)])
        total = total + moved.astype(jnp.float32)
    return total


def tp_gather_rows(block):
    count, rows = lax.axis_size("tp"), block.shape[0]
    whole = jnp.zeros((count * rows, block.shape[1]), block.dtype)
    for k, piece in enumerate(tp_blocks(block)):
        start = lax.rem(lax.axis_index("tp") + k, count) * rows
        whole = lax.dynamic_update_slice_in_dim(whole, piece, start, 0)
    return whole


def tp_scatter_rows(whole, rows):
    count = lax.axis_size("tp")
    return tp_sum(
        [
            lax.dynamic_slice_in_dim(
                whole, lax.rem(lax.axis_index("tp") + k, count) * rows, rows, 0
            )
            for k in range(count)
        ]
    )


def tp_scatter_units(whole, axis):
    return tp_sum(jnp.split(whole.astype(jnp.bfloat16), lax.axis_size("tp"), axis=axis))


def dense_gates(logits, routes, expert_ids):
    hits = jnp.any(routes[:, :, None] == expert_ids[None, None, :], axis=1)
    chosen = jnp.where(hits, logits, -jnp.inf)
    weights = jnp.exp(chosen - jnp.max(chosen, axis=1, keepdims=True))
    return weights / jnp.sum(weights, axis=1, keepdims=True)


def shards(
    tokens,
    gain_attn,
    w_query,
    w_key,
    w_value,
    w_out,
    gain_ffn,
    w_router,
    w_gate,
    w_up,
    w_down,
    segment_ids,
    routes,
    out_grad,
):
    tok_rows, width = tokens.shape
    group_rows = segment_ids.shape[0]
    seq_len = SEQ_LEN
    seq_count = group_rows // seq_len
    query_cols = w_query.shape[1]
    kv_cols = w_key.shape[1]
    head_dim = HEAD
    tp_index = lax.axis_index("tp")
    expert_count = w_router.shape[1]
    capacity = CAP
    top_count = routes.shape[1]
    local_experts = w_gate.shape[0]
    owner_count = lax.axis_size("exp")
    gate_full, up_full, down_full = (
        jnp.concatenate(tp_blocks(w_gate), axis=2),
        jnp.concatenate(tp_blocks(w_up), axis=2),
        jnp.concatenate(tp_blocks(w_down), axis=1),
    )
    exp_index = lax.axis_index("exp")
    routes_all = (
        lax.all_gather(routes.T.astype(jnp.float32), "exp", axis=1, tiled=True)
        .astype(jnp.int32)
        .T
    )
    og_all = lax.all_gather(out_grad, "exp", axis=0, tiled=True)
    own_ids = exp_index * local_experts + jnp.arange(local_experts, dtype=jnp.int32)
    own_hits = jnp.any(
        routes_all.T.reshape(1, top_count, owner_count, tok_rows)
        == own_ids[:, None, None, None],
        axis=1,
    )
    tok_ids = jnp.arange(tok_rows, dtype=jnp.int32)
    earlier = (tok_ids[:, None] < tok_ids[None, :]).astype(jnp.bfloat16)
    ranks = jnp.einsum(
        "usr,rt->ust", own_hits.astype(jnp.bfloat16), earlier, preferred_element_type=jnp.float32
    ).astype(jnp.int32)
    ranks = jnp.where(own_hits, ranks, -1)
    dispatch = (
        ranks[:, :, None, :] == jnp.arange(capacity, dtype=jnp.int32)[None, None, :, None]
    ).astype(jnp.bfloat16)
    og_packed = jnp.einsum(
        "usct,std->uscd",
        dispatch,
        og_all.reshape(owner_count, tok_rows, width),
        preferred_element_type=jnp.float32,
    ).astype(jnp.bfloat16).reshape(local_experts, -1, width)
    source = tokens.astype(jnp.float32)
    scale_one = lax.rsqrt(jnp.mean(source * source, axis=1, keepdims=True) + epsilon)
    unit_one = source * scale_one
    normed = (unit_one * gain_attn).astype(jnp.bfloat16)
    gathered = tp_gather_rows(normed)
    w_proj = jnp.concatenate([w_query, w_key, w_value], axis=1)
    projected = jnp.dot(gathered, w_proj, preferred_element_type=jnp.float32)
    seq_rows = segment_ids.reshape(seq_count, seq_len)
    cos_table, sin_table = rope_tables(doc_positions(seq_rows).reshape(-1), head_dim)
    queries = rotate(
        projected[:, :query_cols].reshape(group_rows, -1, head_dim), cos_table, sin_table
    ).astype(jnp.bfloat16)
    key_rows = rotate(
        projected[:, query_cols : query_cols + kv_cols].reshape(group_rows, -1, head_dim),
        cos_table,
        sin_table,
    ).astype(jnp.bfloat16)
    value_rows = (
        projected[:, query_cols + kv_cols :].astype(jnp.bfloat16).reshape(group_rows, -1, head_dim)
    )
    query_seqs = queries.reshape(seq_count, seq_len, -1, head_dim)
    key_seqs = key_rows.reshape(seq_count, seq_len, -1, head_dim)
    value_seqs = value_rows.reshape(seq_count, seq_len, -1, head_dim)
    attended, log_total = lax.map(attend_forward, (query_seqs, key_seqs, value_seqs, seq_rows))
    head_rows = attended.reshape(group_rows, query_cols).astype(jnp.bfloat16)
    out_local = lax.dynamic_slice_in_dim(w_out, tp_index * query_cols, query_cols, 0)
    part_rows = head_rows
    branch = tp_scatter_rows(
        jnp.dot(part_rows, out_local, preferred_element_type=jnp.float32), tok_rows
    )
    hidden = source + branch
    scale_two = lax.rsqrt(jnp.mean(hidden * hidden, axis=1, keepdims=True) + epsilon)
    unit_two = hidden * scale_two
    normed_ffn = (unit_two * gain_ffn).astype(jnp.bfloat16)
    logits = jnp.dot(normed_ffn, w_router, preferred_element_type=jnp.float32)
    expert_ids = jnp.arange(expert_count, dtype=jnp.int32)
    gates = dense_gates(logits, routes, expert_ids)
    x_send, gate_full, up_full, down_full = lax.optimization_barrier(
        (normed_ffn, gate_full, up_full, down_full)
    )
    x_all = lax.all_gather(x_send, "exp", axis=0, tiled=True).reshape(
        owner_count, tok_rows, width
    )
    logits_all = jnp.einsum("std,de->ste", x_all, w_router, preferred_element_type=jnp.float32)
    gates_all = dense_gates(
        logits_all.reshape(-1, expert_count), routes_all, expert_ids
    ).reshape(owner_count, tok_rows, owner_count, local_experts)
    own_gates = lax.dynamic_index_in_dim(gates_all, exp_index, 2, keepdims=False)
    slot_gates = jnp.einsum(
        "usct,stu->usc", dispatch, own_gates, precision=lax.Precision.HIGHEST,
        preferred_element_type=jnp.float32,
    )
    received = jnp.einsum(
        "usct,std->uscd", dispatch, x_all, preferred_element_type=jnp.float32
    ).astype(jnp.bfloat16).reshape(local_experts, -1, width)
    slot_gates = slot_gates.reshape(local_experts, -1)
    gate_pre = jnp.einsum("umd,udf->umf", received, gate_full, preferred_element_type=jnp.float32)
    up_pre = jnp.einsum("umd,udf->umf", received, up_full, preferred_element_type=jnp.float32)
    sigmoid_gate = jax.nn.sigmoid(gate_pre)
    inner_act = (gate_pre * sigmoid_gate * up_pre).astype(jnp.bfloat16)
    result = jnp.einsum(
        "umf,ufd->umd", inner_act, down_full, preferred_element_type=jnp.float32
    ).astype(jnp.bfloat16).astype(jnp.float32)
    weighted = (slot_gates[..., None] * result).astype(jnp.bfloat16)
    mixture_part = jnp.einsum(
        "usct,uscd->std",
        dispatch,
        weighted.reshape(local_experts, owner_count, capacity, width),
        preferred_element_type=jnp.float32,
    ).astype(jnp.bfloat16)
    og_packed, mixture_part = lax.optimization_barrier((og_packed, mixture_part))
    mixture = lax.psum_scatter(
        mixture_part.reshape(-1, width), "exp", scatter_dimension=0, tiled=True
    ).astype(jnp.float32)
    output = (hidden + mixture).astype(jnp.bfloat16)
    share_slots = jnp.sum(result * og_packed.astype(jnp.float32), axis=2)
    share_back = jnp.einsum(
        "usct,usc->sut", dispatch, share_slots.reshape(local_experts, owner_count, capacity),
        precision=lax.Precision.HIGHEST, preferred_element_type=jnp.float32,
    )
    share_grad = (
        lax.all_to_all(share_back, "exp", split_axis=0, concat_axis=0, tiled=True)
        .reshape(expert_count, tok_rows)
        .T
    )
    arrived = (slot_gates[..., None] * og_packed.astype(jnp.float32)).astype(jnp.bfloat16)
    inner_grad = jnp.einsum("umd,ufd->umf", arrived, down_full, preferred_element_type=jnp.float32)
    gate_grad = (
        inner_grad * up_pre * sigmoid_gate * (1.0 + gate_pre * (1.0 - sigmoid_gate))
    ).astype(jnp.bfloat16)
    up_grad = (inner_grad * gate_pre * sigmoid_gate).astype(jnp.bfloat16)
    back_rows = (
        jnp.einsum("umf,udf->umd", gate_grad, gate_full, preferred_element_type=jnp.float32)
        + jnp.einsum("umf,udf->umd", up_grad, up_full, preferred_element_type=jnp.float32)
    ).astype(jnp.bfloat16)
    grad_part = jnp.einsum(
        "usct,uscd->std",
        dispatch,
        back_rows.reshape(local_experts, owner_count, capacity, width),
        preferred_element_type=jnp.float32,
    ).astype(jnp.bfloat16)
    ffn_grad = lax.psum_scatter(
        grad_part.reshape(-1, width), "exp", scatter_dimension=0, tiled=True
    ).astype(jnp.float32)
    down_part = jnp.einsum("umf,umd->ufd", inner_act, arrived, preferred_element_type=jnp.float32)
    gate_part = jnp.einsum("umd,umf->udf", received, gate_grad, preferred_element_type=jnp.float32)
    up_part = jnp.einsum("umd,umf->udf", received, up_grad, preferred_element_type=jnp.float32)
    logit_grad = (
        gates * (share_grad - jnp.sum(gates * share_grad, axis=1, keepdims=True))
    ).astype(jnp.bfloat16)
    router_part = contract(normed_ffn, logit_grad, 0, 0)
    ffn_grad = ffn_grad + contract(logit_grad, w_router, 1, 1)
    ffn_part = jnp.sum(ffn_grad * unit_two, axis=0)
    unit_grad_two = ffn_grad * gain_ffn
    hidden_grad = out_grad.astype(jnp.float32) + scale_two * (
        unit_grad_two - unit_two * jnp.mean(unit_grad_two * unit_two, axis=1, keepdims=True)
    )
    branch_low = hidden_grad.astype(jnp.bfloat16)
    part_rows = tp_gather_rows(branch_low)
    update = contract(part_rows, out_local, 1, 1)
    grads_heads = update
    grads_heads, out_rows = (grads_heads, contract(head_rows, part_rows, 0, 0))
    head_grad = grads_heads.astype(jnp.bfloat16)
    out_weight_grad = lax.all_gather(
        lax.psum_scatter(
            out_rows.astype(jnp.bfloat16), "exp", scatter_dimension=0, tiled=True
        ),
        ("tp", "exp"),
        axis=0,
        tiled=True,
    ).astype(jnp.float32)
    query_grad, key_grad, value_grad = lax.map(
        attend_backward,
        (
            query_seqs,
            key_seqs,
            value_seqs,
            seq_rows,
            log_total,
            head_grad.reshape(seq_count, seq_len, query_cols),
        ),
    )
    query_grad = rotate_back(query_grad.reshape(group_rows, -1, head_dim), cos_table, sin_table)
    key_grad = rotate_back(key_grad.reshape(group_rows, -1, head_dim), cos_table, sin_table)
    proj_grad = jnp.concatenate(
        [
            query_grad.reshape(group_rows, -1),
            key_grad.reshape(group_rows, -1),
            value_grad.reshape(group_rows, -1),
        ],
        axis=1,
    ).astype(jnp.bfloat16)
    proj_part = contract(gathered, proj_grad, 0, 0)
    part_rows = proj_grad
    normed_grad = tp_scatter_rows(
        contract(part_rows, w_proj, 1, 1).astype(jnp.bfloat16), tok_rows
    )
    attn_part = jnp.sum(normed_grad * unit_one, axis=0)
    unit_grad_one = normed_grad * gain_attn
    input_grad = hidden_grad + scale_one * (
        unit_grad_one - unit_one * jnp.mean(unit_grad_one * unit_one, axis=1, keepdims=True)
    )
    gate_weight_grad, up_weight_grad, down_weight_grad = (
        tp_scatter_units(gate_part, 2),
        tp_scatter_units(up_part, 2),
        tp_scatter_units(down_part, 1),
    )
    proj_low, output = lax.optimization_barrier((proj_part.astype(jnp.bfloat16), output))
    proj_sum = lax.all_gather(
        lax.psum_scatter(proj_low, "exp", scatter_dimension=0, tiled=True),
        "exp",
        axis=0,
        tiled=True,
    ).astype(jnp.float32)
    query_weight_grad, key_weight_grad, value_weight_grad = (
        proj_sum[:, :query_cols],
        proj_sum[:, query_cols : query_cols + kv_cols],
        proj_sum[:, query_cols + kv_cols :],
    )
    attn_gain_grad = jnp.sum(
        lax.all_gather(attn_part[None, :], ("exp", "tp"), axis=0, tiled=True), axis=0
    )
    small = lax.psum(jnp.concatenate([router_part, ffn_part[:, None]], axis=1), ("exp", "tp"))
    router_grad, ffn_gain_grad = small[:, :expert_count], small[:, expert_count]
    return (
        output,
        input_grad,
        attn_gain_grad,
        query_weight_grad,
        key_weight_grad,
        value_weight_grad,
        out_weight_grad,
        ffn_gain_grad,
        router_grad,
        gate_weight_grad,
        up_weight_grad,
        down_weight_grad,
    )


def solution(mesh):
    in_specs = (
        P(("exp", "tp"), None),
        P(),
        P(None, "tp"),
        P(None, "tp"),
        P(None, "tp"),
        P(),
        P(),
        P(),
        P("exp", None, "tp"),
        P("exp", None, "tp"),
        P("exp", "tp", None),
        P("exp"),
        P(("exp", "tp"), None),
        P(("exp", "tp"), None),
    )
    out_specs = (
        P(("exp", "tp"), None),
        P(("exp", "tp"), None),
        P(),
        P(None, "tp"),
        P(None, "tp"),
        P(None, "tp"),
        P(),
        P(),
        P(),
        P("exp", None, "tp"),
        P("exp", None, "tp"),
        P("exp", "tp", None),
    )
    return jax.shard_map(shards, mesh=mesh, in_specs=in_specs, out_specs=out_specs, check_vma=False)
```
